32 devices in a mesh: row: 16 (over z, x, core), col: 2 (over y).
Axes of the slice: x: 2, y: 2, z: 4, core: 2. Of those that a mesh axis runs over, the one named last changes fastest.
Arguments:
- first_homolog_embedding: bfloat16 [128, 512, 32], P(None, ('row', 'col')), may hold values from -12 to 12
- second_homolog_embedding: bfloat16 [128, 512, 32], P(None, ('row', 'col')), may hold values from -12 to 12
- token_chain_index: int32 [512], replicated, may hold values from 0 to 7, never falling along the last dimension, each value on 1 to 192 neighbouring positions
- incoming_pair_state: bfloat16 [512, 512, 128], P('row', 'col'), may hold values from -6 to 6
- tensor_mixing_matrix: bfloat16 [1024, 128], replicated, may hold values from -0.1875 to 0.1875
- outer_product_bias: float32 [128], replicated, may hold values from -3 to 3
- transition_norm_gain: float32 [128], replicated, may hold values from 0.5 to 1.5
- transition_gate_weight: bfloat16 [128, 512], replicated, may hold values from -0.5 to 0.5
- transition_up_weight: bfloat16 [128, 512], replicated, may hold values from -0.5 to 0.5
- transition_down_weight: bfloat16 [512, 128], replicated, may hold values from -0.25 to 0.25
- distogram_weight: bfloat16 [128, 64], replicated, may hold values from -0.5 to 0.5
- distogram_bias: float32 [64], replicated, may hold values from -3 to 3
Outputs:
- pair_out: bfloat16 [512, 512, 128], P('row', 'col')
- logits: float32 [64, 512, 512], P(None, 'row', 'col')
The draws below stay inside these ranges and needn't reach their ends.
Inputs may be any that keep to these rules, and one draw needn't show every extreme that they name: `token_chain_index`: chain numbers never fall along the tokens; each chain has 1 to 192 tokens and one chain has exactly 192.
All inputs are finite; a program needn't handle non-finite values.
Results may differ from the reference program's by a relative error of at most 0.006.
Values may be sent and summed in bfloat16 or wider, within the bound.
A program may use at most 64 MiB of HBM per device.

```python
import math
import jax
import jax.numpy as jnp
import numpy as np
from jax import lax

FEATURE_DEPTH = 32
EDGE_FEATURES = 128
HID = 512
BINS = 64
SLAB = 64
CHAINS = 8
RESIDUE_WINDOW = 512
HOMOLOG_NUMBER = 128
LONGEST = 192


def block_levels(rng, shape, shards, low, largest):
    factor_of = 1.0
    for position, blocks in shards:
        heights = jax.random.uniform(jax.random.fold_in(jax.random.fold_in(rng, 6), position), (blocks,), jnp.float32, low / len(shards), largest / len(shards))
        factor_of = factor_of * jnp.repeat(jnp.exp(heights), shape[position] // blocks).reshape((-1,) + (1,) * (len(shape) - 1 - position))
    return factor_of


def length_profile(count, total, limit, slope):
    portions = [(1 << 20) // math.isqrt(rank ** slope) + 1 for rank in range(2, count + 1)]
    rest, counts = total - limit - (count - 1), [1] * (count - 1)
    while rest > 0:
        movable = [i for i in range(count - 1) if counts[i] < limit]
        whole, budget = sum([portions[i] for i in movable]), rest
        for i in movable:
            more = min(limit - counts[i], max(1, budget * portions[i] // whole), rest)
            counts[i] = counts[i] + more
            rest = rest - more
    return np.array([limit] + counts)


def uneven(own_key, number_of, total, most, slope):
    if number_of == 2:
        one = jax.random.randint(own_key, (), max(1, total - most), min(most, total - 1) + 1)
        return jnp.stack([one, total - one])
    sizes = jnp.asarray(length_profile(number_of, total, most, slope), jnp.int32)
    couples = (number_of - 1) // 2
    source_of, receiver = sizes[1:1 + 2 * couples:2], sizes[2:2 + 2 * couples:2]
    room = jnp.minimum(source_of - 1, most - receiver)
    passed = jax.random.randint(jax.random.fold_in(own_key, 1), (couples,), 0, 1 << 20) % (room + 1)
    sizes = sizes.at[1:1 + 2 * couples:2].set(source_of - passed).at[2:2 + 2 * couples:2].set(receiver + passed)
    return sizes[jax.random.permutation(jax.random.fold_in(own_key, 2), number_of)]


def normal_values(own_key, dims, scale, bound, shards=(), held_as=jnp.bfloat16):
    array = scale * jax.random.normal(own_key, dims, jnp.float32)
    if shards:
        array = array * block_levels(own_key, dims, shards, -0.22, 0.18)
    return jnp.clip(array, -bound, bound).astype(held_as)


def setup_inputs(seed: int = 0) -> dict:
    streams_of = jax.random.split(jax.random.key(seed), 13)
    first_homolog_embedding = normal_values(streams_of[0], (HOMOLOG_NUMBER, RESIDUE_WINDOW, FEATURE_DEPTH), 2.0, 12.0, ((1, 32),))
    second_homolog_embedding = normal_values(streams_of[1], (HOMOLOG_NUMBER, RESIDUE_WINDOW, FEATURE_DEPTH), 2.0, 12.0, ((1, 32),))
    token_chain_index = jnp.searchsorted(jnp.cumsum(uneven(streams_of[2], CHAINS, RESIDUE_WINDOW, LONGEST, 2)), jnp.arange(RESIDUE_WINDOW), side="right").astype(jnp.int32)
    incoming_pair_state = normal_values(streams_of[3], (RESIDUE_WINDOW, RESIDUE_WINDOW, EDGE_FEATURES), 1.0, 6.0, ((0, 16), (1, 2)))
    tensor_mixing_matrix = normal_values(streams_of[4], (FEATURE_DEPTH * FEATURE_DEPTH, EDGE_FEATURES), (FEATURE_DEPTH * FEATURE_DEPTH) ** -0.5, 0.1875)
    outer_product_bias = normal_values(streams_of[5], (EDGE_FEATURES,), 0.5, 3.0, (), jnp.float32)
    transition_norm_gain = jnp.clip(1.0 + 0.1 * jax.random.normal(streams_of[6], (EDGE_FEATURES,), jnp.float32), 0.5, 1.5)
    transition_gate_weight = normal_values(streams_of[7], (EDGE_FEATURES, HID), EDGE_FEATURES ** -0.5, 0.5)
    transition_up_weight = normal_values(streams_of[8], (EDGE_FEATURES, HID), EDGE_FEATURES ** -0.5, 0.5)
    transition_down_weight = normal_values(streams_of[9], (HID, EDGE_FEATURES), HID ** -0.5, 0.25)
    distogram_weight = normal_values(streams_of[10], (EDGE_FEATURES, BINS), EDGE_FEATURES ** -0.5, 0.5)
    distogram_bias = normal_values(streams_of[11], (BINS,), 0.5, 3.0, (), jnp.float32)
    return {"first_homolog_embedding": first_homolog_embedding, "second_homolog_embedding": second_homolog_embedding, "token_chain_index": token_chain_index, "incoming_pair_state": incoming_pair_state, "tensor_mixing_matrix": tensor_mixing_matrix, "outer_product_bias": outer_product_bias, "transition_norm_gain": transition_norm_gain, "transition_gate_weight": transition_gate_weight, "transition_up_weight": transition_up_weight, "transition_down_weight": transition_down_weight, "distogram_weight": distogram_weight, "distogram_bias": distogram_bias}


def layer_norm(values, transition_norm_gain):
    center = lax.optimization_barrier(jnp.mean(values, axis=-1, keepdims=True))
    shifted = values - center
    spread = lax.optimization_barrier(jnp.mean(shifted * shifted, axis=-1, keepdims=True))
    return shifted * lax.rsqrt(spread + 1e-05) * transition_norm_gain.astype(jnp.float32)

def transition_rows(mid_rows, transition_norm_gain, transition_gate_weight, transition_up_weight, transition_down_weight):
    mid_float = mid_rows.astype(jnp.float32)
    normed = layer_norm(mid_float, transition_norm_gain).astype(jnp.bfloat16)
    gate_pre = jnp.dot(normed, transition_gate_weight, preferred_element_type=jnp.float32)
    up_pre = jnp.dot(normed, transition_up_weight, preferred_element_type=jnp.float32)
    hidden = (jax.nn.silu(gate_pre) * up_pre).astype(jnp.bfloat16)
    result = mid_float + jnp.dot(hidden, transition_down_weight, preferred_element_type=jnp.float32)
    return result.astype(jnp.bfloat16)

def reference(first_homolog_embedding, second_homolog_embedding, token_chain_index, incoming_pair_state, tensor_mixing_matrix, outer_product_bias, transition_norm_gain, transition_gate_weight, transition_up_weight, transition_down_weight, distogram_weight, distogram_bias):
    grid_piece = 8
    block_count = RESIDUE_WINDOW // grid_piece
    left_single_precision = first_homolog_embedding.astype(jnp.float32)
    right_single_precision = second_homolog_embedding.astype(jnp.float32)

    def pair_block(block_index):
        row_start = (block_index * grid_piece).astype(jnp.int32)
        left_sequence_rows = lax.dynamic_slice_in_dim(left_single_precision, row_start, grid_piece, 1)
        chain_rows = lax.dynamic_slice_in_dim(token_chain_index, row_start, grid_piece, 0)
        same_chain = (chain_rows[:, None] == token_chain_index[None, :]).astype(jnp.float32)
        paired_sum = jnp.einsum('sic,sjd->ijcd', left_sequence_rows[:SLAB], right_single_precision[:SLAB])
        unpaired_sum = jnp.einsum('sic,sjd->ijcd', left_sequence_rows[SLAB:], right_single_precision[SLAB:])
        weight = same_chain[:, :, None, None]
        homolog_mean = (paired_sum + weight * unpaired_sum) / (SLAB * (1.0 + weight))
        raveled_matrix = homolog_mean.astype(jnp.bfloat16).reshape(grid_piece * RESIDUE_WINDOW, FEATURE_DEPTH * FEATURE_DEPTH)
        inputs = lax.dynamic_slice_in_dim(incoming_pair_state, row_start, grid_piece, 0).reshape(grid_piece * RESIDUE_WINDOW, EDGE_FEATURES)
        middle = jnp.dot(raveled_matrix, tensor_mixing_matrix, preferred_element_type=jnp.float32)
        middle = middle + outer_product_bias.astype(jnp.float32) + inputs.astype(jnp.float32)
        middle = middle.astype(jnp.bfloat16)
        updated = transition_rows(middle, transition_norm_gain, transition_gate_weight, transition_up_weight, transition_down_weight)
        projected = jnp.dot(updated, distogram_weight, preferred_element_type=jnp.float32).astype(jnp.bfloat16)
        return (updated.reshape(grid_piece, RESIDUE_WINDOW, EDGE_FEATURES), projected.reshape(grid_piece, RESIDUE_WINDOW, BINS))
    pair_blocks, proj_blocks = lax.map(pair_block, jnp.arange(block_count, dtype=jnp.int32))
    pair_out = pair_blocks.reshape(RESIDUE_WINDOW, RESIDUE_WINDOW, EDGE_FEATURES)
    projected = proj_blocks.reshape(RESIDUE_WINDOW, RESIDUE_WINDOW, BINS)
    logits = jnp.transpose(projected, (2, 0, 1)).astype(jnp.float32)
    logits = logits + jnp.transpose(projected, (2, 1, 0)).astype(jnp.float32)
    logits = logits + distogram_bias.astype(jnp.float32)[:, None, None]
    return (pair_out, logits)
```

```python
import functools

import jax
import jax.numpy as jnp
from jax import lax
from jax.experimental import pallas as pl
from jax.experimental.pallas import tpu as pltpu
from jax.sharding import PartitionSpec as P

MESH = pl.DeviceIdType.MESH
VMEM_BYTES = 56 * 1024 * 1024


def pair_kernel(
    slab,
    width,
    group,
    rows_tile,
    chain_rows,
    chain_cols,
    left,
    right,
    incoming,
    mixing,
    bias,
    gain,
    gate_up,
    down,
    bins_weight,
    pair_out,
    own_bins,
    turned_bins,
    lhs,
    weights,
    outer,
    bins,
):
    step = pl.program_id(0)
    cols_tile = right.shape[1]
    sequences = 2 * slab
    channels = mixing.shape[0]
    hid = down.shape[1]
    bins_count = bins_weight.shape[0]
    sides, _, lanes = bins.shape
    first_row = step * group
    first_chain = chain_rows[first_row]
    last_chain = chain_rows[first_row + group - 1]

    def load_chains(low):
        lane = lax.broadcasted_iota(jnp.int32, (cols_tile, sequences), 1)
        apart = jnp.where(lane < slab, 1.0 / slab, 0.0).astype(jnp.float32)
        for half in range(2):
            chain = low + half
            same = chain_cols[...] == chain
            weights[:, half * sequences : (half + 1) * sequences] = jnp.where(
                same, 0.5 / slab, apart
            ).astype(jnp.bfloat16)
            for row in range(group):
                keep = jnp.where(chain_rows[first_row + row] == chain, 1.0, 0.0)
                lhs[row * width : (row + 1) * width, half * sequences : (half + 1) * sequences] = (
                    left[row * width : (row + 1) * width, :].astype(jnp.float32) * keep
                ).astype(jnp.bfloat16)

    def outer_part(depth):
        block = right[depth]
        spread = jnp.concatenate([block, block], axis=1) * weights[...]
        part = lax.dot_general(
            lhs[...], spread, (((1,), (1,)), ((), ())), preferred_element_type=jnp.float32
        )
        return part.astype(jnp.bfloat16).reshape(group, width, cols_tile)

    def place(depth):
        return pl.ds(pl.multiple_of(depth * width, width), width)

    load_chains(first_chain)

    @pl.loop(0, width, unroll=4)
    def _(depth):
        outer[:, place(depth), :] = outer_part(depth)

    @pl.loop(1, (last_chain - first_chain) // 2 + 1)
    def _(turn):
        load_chains(first_chain + 2 * turn)

        @pl.loop(0, width)
        def _(depth):
            outer[:, place(depth), :] = outer[:, place(depth), :] + outer_part(depth)

    def one_row(row):
        mid = jnp.dot(mixing[...], outer[row], preferred_element_type=jnp.float32)
        mid = mid + bias[...] + incoming[row].astype(jnp.float32).T
        mid = mid.astype(jnp.bfloat16).astype(jnp.float32)
        center = jnp.mean(mid, axis=0, keepdims=True)
        shifted = mid - center
        spread = jnp.mean(shifted * shifted, axis=0, keepdims=True)
        normed = (shifted * lax.rsqrt(spread + 1e-05) * gain[...]).astype(jnp.bfloat16)
        both = jnp.dot(gate_up[...], normed, preferred_element_type=jnp.float32)
        half_gate = 0.5 * both[:hid]
        hidden = ((half_gate + half_gate * jnp.tanh(half_gate)) * both[hid:]).astype(jnp.bfloat16)
        result = mid + jnp.dot(down[...], hidden, preferred_element_type=jnp.float32)
        rounded = result.astype(jnp.bfloat16)
        pair_out[row] = result.T.astype(jnp.bfloat16)
        projected = jnp.dot(bins_weight[...], rounded, preferred_element_type=jnp.float32)
        for side in range(sides):
            bins[side, pl.ds(first_row + row, bins_count, stride=rows_tile), :] = projected[
                :, side * lanes : (side + 1) * lanes
            ]

    @pl.loop(0, group // 2)
    def _(pair):
        for half in range(2):
            one_row(2 * pair + half)

    @pl.when(step == pl.num_programs(0) - 1)
    def _():
        for side in range(sides):
            columns = slice(side * lanes, (side + 1) * lanes)
            own_bins[:, :, columns] = (
                bins[side].astype(jnp.bfloat16).reshape(bins_count, rows_tile, lanes)
            )
            for part in range(turned_bins.shape[0]):
                turned_bins[part, columns, :] = bins[
                    side, part * lanes : (part + 1) * lanes, :
                ].T.astype(jnp.bfloat16)


def exchange_kernel(
    row_groups, rows_tile, turned_bins, own_bins, bias, logits, landed, send_sem, recv_sem, own_sem
):
    row_at = lax.axis_index("row")
    col_at = lax.axis_index("col")
    mine = lax.rem(row_at, row_groups)
    peer_col = row_at // row_groups
    inside = peer_col == col_at

    def remote(slot):
        return jnp.logical_or(jnp.logical_not(inside), slot != mine)

    def peer(slot):
        return (col_at * row_groups + slot, peer_col)

    def block(slot):
        return turned_bins.at[:, pl.ds(pl.multiple_of(slot * rows_tile, rows_tile), rows_tile), :]

    def copy(slot):
        return pltpu.make_async_remote_copy(
            src_ref=block(slot),
            dst_ref=landed.at[mine],
            send_sem=send_sem.at[slot],
            recv_sem=recv_sem.at[mine],
            device_id=peer(slot),
            device_id_type=MESH,
        )

    def arrival(slot):
        return pltpu.make_async_remote_copy(
            src_ref=block(slot),
            dst_ref=landed.at[slot],
            send_sem=send_sem.at[slot],
            recv_sem=recv_sem.at[slot],
            device_id=peer(slot),
            device_id_type=MESH,
        )

    barrier = pltpu.get_barrier_semaphore()
    for slot in range(row_groups):

        @pl.when(remote(slot))
        def _():
            pl.semaphore_signal(barrier, inc=1, device_id=peer(slot), device_id_type=MESH)

    pl.semaphore_wait(barrier, jnp.where(inside, row_groups - 1, row_groups))

    for turn in range(row_groups):
        slot = lax.rem(mine + turn, row_groups)

        @pl.when(remote(slot))
        def _():
            copy(slot).start()

    @pl.when(inside)
    def _():
        local = pltpu.make_async_copy(block(mine), landed.at[mine], own_sem)
        local.start()
        local.wait()

    for turn in range(row_groups):
        slot = lax.rem(mine + turn, row_groups)

        @pl.when(remote(slot))
        def _():
            arrival(slot).wait_recv()
            copy(slot).wait_send()

    parts, lanes = landed.shape[1], landed.shape[3]
    each = lanes // rows_tile

    @pl.loop(0, parts)
    def _(part):
        got = [landed[slot, part].astype(jnp.float32) for slot in range(row_groups)]
        for inner in range(each):
            mirrored = jnp.concatenate(
                [one[:, inner * rows_tile : (inner + 1) * rows_tile] for one in got], axis=1
            )
            at = part * each + inner
            logits[at] = own_bins[at].astype(jnp.float32) + mirrored + bias[at]


def per_device(
    first_homolog_embedding,
    second_homolog_embedding,
    token_chain_index,
    incoming_pair_state,
    tensor_mixing_matrix,
    outer_product_bias,
    transition_norm_gain,
    transition_gate_weight,
    transition_up_weight,
    transition_down_weight,
    distogram_weight,
    distogram_bias,
):
    row_count = lax.axis_size("row")
    col_count = lax.axis_size("col")
    row_at = lax.axis_index("row")
    col_at = lax.axis_index("col")
    rows_tile, cols_tile, channels = incoming_pair_state.shape
    sequences, tokens_local, width = first_homolog_embedding.shape
    hid = transition_gate_weight.shape[1]
    bins_count = distogram_weight.shape[1]
    row_groups = row_count // col_count
    slab = sequences // 2
    f32, bf16 = jnp.float32, jnp.bfloat16

    left = lax.all_gather(
        jnp.transpose(first_homolog_embedding, (1, 2, 0)), "col", axis=0, tiled=True
    ).reshape(rows_tile * width, sequences)
    right = lax.all_gather(
        jnp.transpose(second_homolog_embedding, (1, 2, 0)), ("row", "col"), axis=0, tiled=True
    )
    right = lax.dynamic_slice_in_dim(right, col_at * cols_tile, cols_tile, 0)
    right = jnp.transpose(right, (1, 0, 2))

    chain_rows = lax.dynamic_slice_in_dim(token_chain_index, row_at * rows_tile, rows_tile, 0)
    chain_cols = lax.dynamic_slice_in_dim(token_chain_index, col_at * cols_tile, cols_tile, 0)
    chain_cols = jnp.broadcast_to(chain_cols[:, None], (cols_tile, sequences))
    mixing = jnp.transpose(
        tensor_mixing_matrix.reshape(width, width, channels), (2, 1, 0)
    ).reshape(channels, width * width)
    bias = jnp.broadcast_to(outer_product_bias[:, None], (channels, cols_tile))
    gain = jnp.broadcast_to(transition_norm_gain[:, None], (channels, cols_tile))
    gate_up = jnp.concatenate([transition_gate_weight.T, transition_up_weight.T], axis=0)

    group = min(16, rows_tile)
    lanes = 128
    parts = bins_count * rows_tile // lanes

    def whole(*shape):
        return pl.BlockSpec(shape, lambda step: (0,) * len(shape))

    pair_out, own_bins, turned_bins = pl.pallas_call(
        functools.partial(pair_kernel, slab, width, group, rows_tile),
        grid=(rows_tile // group,),
        in_specs=[
            pl.BlockSpec(memory_space=pltpu.SMEM),
            whole(cols_tile, sequences),
            pl.BlockSpec((group * width, sequences), lambda step: (step, 0)),
            whole(width, cols_tile, sequences),
            pl.BlockSpec((group, cols_tile, channels), lambda step: (step, 0, 0)),
            whole(channels, width * width),
            whole(channels, cols_tile),
            whole(channels, cols_tile),
            whole(2 * hid, channels),
            whole(channels, hid),
            whole(bins_count, channels),
        ],
        out_specs=[
            pl.BlockSpec((group, cols_tile, channels), lambda step: (step, 0, 0)),
            whole(bins_count, rows_tile, cols_tile),
            whole(parts, cols_tile, lanes),
        ],
        out_shape=[
            jax.ShapeDtypeStruct((rows_tile, cols_tile, channels), bf16),
            jax.ShapeDtypeStruct((bins_count, rows_tile, cols_tile), bf16),
            jax.ShapeDtypeStruct((parts, cols_tile, lanes), bf16),
        ],
        scratch_shapes=[
            pltpu.VMEM((group * width, 2 * sequences), bf16),
            pltpu.VMEM((cols_tile, 2 * sequences), bf16),
            pltpu.VMEM((group, width * width, cols_tile), bf16),
            pltpu.VMEM((cols_tile // lanes, bins_count * rows_tile, lanes), f32),
        ],
        compiler_params=pltpu.CompilerParams(vmem_limit_bytes=VMEM_BYTES),
        name="pair_tile",
    )(
        chain_rows,
        chain_cols,
        left,
        right,
        incoming_pair_state,
        mixing,
        bias,
        gain,
        gate_up,
        transition_down_weight.T,
        distogram_weight.T,
    )

    vmem = pl.BlockSpec(memory_space=pltpu.VMEM)
    logits = pl.pallas_call(
        functools.partial(exchange_kernel, row_groups, rows_tile),
        in_specs=[vmem, vmem, pl.BlockSpec(memory_space=pltpu.SMEM)],
        out_specs=vmem,
        out_shape=jax.ShapeDtypeStruct((bins_count, rows_tile, cols_tile), f32),
        scratch_shapes=[
            pltpu.VMEM((row_groups, parts, rows_tile, lanes), bf16),
            pltpu.SemaphoreType.DMA((row_groups,)),
            pltpu.SemaphoreType.DMA((row_groups,)),
            pltpu.SemaphoreType.DMA,
        ],
        compiler_params=pltpu.CompilerParams(
            collective_id=0, has_side_effects=True, vmem_limit_bytes=VMEM_BYTES
        ),
        name="mirror_bins",
    )(turned_bins, own_bins, distogram_bias)
    return (pair_out, logits)


def solution(mesh):
    placed = (
        P(None, ("row", "col"), None),
        P(None, ("row", "col"), None),
        P(),
        P("row", "col", None),
        P(),
        P(),
        P(),
        P(),
        P(),
        P(),
        P(),
        P(),
    )
    return jax.shard_map(
        per_device,
        mesh=mesh,
        in_specs=placed,
        out_specs=(P("row", "col", None), P(None, "row", "col")),
        check_vma=False,
    )
```

```python
import functools

import jax
import jax.numpy as jnp
from jax import lax
from jax.experimental import pallas as pl
from jax.experimental.pallas import tpu as pltpu
from jax.sharding import PartitionSpec as P

MESH = pl.DeviceIdType.MESH
VMEM_BYTES = 56 * 1024 * 1024


def pair_kernel(
    slab,
    width,
    group,
    rows_tile,
    chain_rows,
    chain_cols,
    left,
    right,
    incoming,
    mixing,
    bias,
    gain,
    gate_up,
    down,
    bins_weight,
    pair_out,
    own_bins,
    turned_bins,
    lhs,
    weights,
    outer,
    bins,
):
    step = pl.program_id(0)
    cols_tile = chain_cols.shape[0]
    sequences = 2 * slab
    channels = mixing.shape[0]
    hid = down.shape[1]
    bins_count = bins_weight.shape[0]
    sides, _, lanes = bins.shape
    first_row = step * group
    first_chain = chain_rows[first_row]
    last_chain = chain_rows[first_row + group - 1]

    def load_chains(low):
        lane = lax.broadcasted_iota(jnp.int32, (cols_tile, sequences), 1)
        apart = jnp.where(lane < slab, 1.0 / slab, 0.0).astype(jnp.float32)
        for half in range(2):
            chain = low + half
            same = chain_cols[...] == chain
            weights[:, half * sequences : (half + 1) * sequences] = jnp.where(
                same, 0.5 / slab, apart
            ).astype(jnp.bfloat16)
            for row in range(group):
                keep = jnp.where(chain_rows[first_row + row] == chain, 1.0, 0.0)
                lhs[row * width : (row + 1) * width, half * sequences : (half + 1) * sequences] = (
                    left[row * width : (row + 1) * width, :].astype(jnp.float32) * keep
                ).astype(jnp.bfloat16)

    def outer_part(depth):
        tokens = right.shape[1] // width
        block = right[:, pl.ds(pl.multiple_of(depth * tokens, tokens), tokens), :]
        block = block.reshape(cols_tile, sequences)
        spread = jnp.concatenate([block, block], axis=1) * weights[...]
        part = lax.dot_general(
            lhs[...], spread, (((1,), (1,)), ((), ())), preferred_element_type=jnp.float32
        )
        return part.astype(jnp.bfloat16).reshape(group, width, cols_tile)

    def place(depth):
        return pl.ds(pl.multiple_of(depth * width, width), width)

    load_chains(first_chain)

    @pl.loop(0, width, unroll=8)
    def _(depth):
        outer[:, place(depth), :] = outer_part(depth)

    @pl.loop(1, (last_chain - first_chain) // 2 + 1)
    def _(turn):
        load_chains(first_chain + 2 * turn)

        @pl.loop(0, width)
        def _(depth):
            outer[:, place(depth), :] = outer[:, place(depth), :] + outer_part(depth)

    def one_row(row):
        mid = jnp.dot(mixing[...], outer[row], preferred_element_type=jnp.float32)
        mid = mid + bias[...] + incoming[row].astype(jnp.float32).T
        mid = mid.astype(jnp.bfloat16).astype(jnp.float32)
        center = jnp.mean(mid, axis=0, keepdims=True)
        shifted = mid - center
        spread = jnp.mean(shifted * shifted, axis=0, keepdims=True)
        normed = (shifted * lax.rsqrt(spread + 1e-05) * gain[...]).astype(jnp.bfloat16)
        both = jnp.dot(gate_up[...], normed, preferred_element_type=jnp.float32)
        half_gate = 0.5 * both[:hid]
        hidden = ((half_gate + half_gate * jnp.tanh(half_gate)) * both[hid:]).astype(jnp.bfloat16)
        result = mid + jnp.dot(down[...], hidden, preferred_element_type=jnp.float32)
        rounded = result.astype(jnp.bfloat16)
        pair_out[row] = result.T.astype(jnp.bfloat16)
        projected = jnp.dot(bins_weight[...], rounded, preferred_element_type=jnp.float32)
        for side in range(sides):
            bins[side, pl.ds(first_row + row, bins_count, stride=rows_tile), :] = projected[
                :, side * lanes : (side + 1) * lanes
            ]

    @pl.loop(0, group // 4)
    def _(quad):
        for part in range(4):
            one_row(4 * quad + part)

    @pl.when(step == pl.num_programs(0) - 1)
    def _():
        for side in range(sides):
            columns = slice(side * lanes, (side + 1) * lanes)
            own_bins[:, :, columns] = (
                bins[side].astype(jnp.bfloat16).reshape(bins_count, rows_tile, lanes)
            )
            for part in range(turned_bins.shape[0]):
                turned_bins[part, columns, :] = bins[
                    side, part * lanes : (part + 1) * lanes, :
                ].T.astype(jnp.bfloat16)


def gather_kernel(
    row_groups,
    col_count,
    first,
    second,
    left,
    right,
    crossed,
    left_send,
    left_recv,
    cross_send,
    cross_recv,
    swap_send,
    swap_recv,
    group_send,
    group_recv,
    core_send,
    core_recv,
    own_sem,
):
    row_at = lax.axis_index("row")
    col = lax.axis_index("col")
    group = row_at // row_groups
    place = lax.rem(row_at, row_groups)
    partner = place + 1 - 2 * lax.rem(place, 2)

    def device(to_group, to_place, to_col):
        return (to_group * row_groups + to_place, to_col)

    def other(step, at):
        return lax.rem(at + step, col_count)

    def in_group(step):
        return lax.rem(place + 2 * step, row_groups)

    def remote(src, dst, send, recv, target):
        return pltpu.make_async_remote_copy(
            src_ref=src,
            dst_ref=dst,
            send_sem=send,
            recv_sem=recv,
            device_id=target,
            device_id_type=MESH,
        )

    def run(at):
        return right.at[pl.ds(at * col_count, col_count)]

    across = range(1, col_count)
    around = range(1, row_groups // 2)
    barrier = pltpu.get_barrier_semaphore()
    for step in across:
        for target in (device(other(step, group), place, col), device(group, place, other(step, col))):
            pl.semaphore_signal(barrier, inc=1, device_id=target, device_id_type=MESH)
    for step in around:
        pl.semaphore_signal(
            barrier, inc=1, device_id=device(group, in_group(step), col), device_id_type=MESH
        )
    pl.semaphore_signal(
        barrier, inc=1, device_id=device(group, partner, col), device_id_type=MESH
    )
    pl.semaphore_wait(barrier, 2 * (col_count - 1) + row_groups // 2)

    def cross(step):
        to = other(step, group)
        return remote(
            second, crossed.at[group], cross_send.at[to], cross_recv.at[group], device(to, place, col)
        )

    def crossing(source):
        return remote(
            second,
            crossed.at[source],
            cross_send.at[source],
            cross_recv.at[source],
            device(source, place, col),
        )

    def left_copy(step, at):
        to = other(step, col)
        return remote(
            first, left.at[at], left_send.at[to], left_recv.at[at], device(group, place, to)
        )

    def swap(step, at):
        to = other(step, col)
        return remote(
            crossed.at[to],
            right.at[place * col_count + at],
            swap_send.at[to],
            swap_recv.at[at],
            device(group, place, to),
        )

    def share(step, at):
        to = in_group(step)
        return remote(
            run(at), run(at), group_send.at[to], group_recv.at[at], device(group, to, col)
        )

    def hand(mine, theirs):
        return remote(
            run(mine),
            run(theirs),
            core_send.at[mine],
            core_recv.at[theirs],
            device(group, partner, col),
        )

    for step in across:
        cross(step).start()
    own = pltpu.make_async_copy(second, crossed.at[group], own_sem.at[0])
    own.start()
    own_left = pltpu.make_async_copy(first, left.at[col], own_sem.at[1])
    own_left.start()
    own.wait()
    own_left.wait()
    for step in across:
        left_copy(step, col).start()

    for step in range(col_count):
        wanted = other(step, group)
        if step:
            crossing(wanted).wait_recv()

        @pl.when(wanted != col)
        def _():
            remote(
                crossed.at[wanted],
                right.at[place * col_count + col],
                swap_send.at[wanted],
                swap_recv.at[col],
                device(group, place, wanted),
            ).start()

        @pl.when(wanted == col)
        def _():
            kept = pltpu.make_async_copy(
                crossed.at[wanted], right.at[place * col_count + col], own_sem.at[2]
            )
            kept.start()
            kept.wait()

    for step in across:
        swap(step, other(step, col)).wait_recv()
    for step in around:
        share(step, place).start()
    hand(place, place).start()
    for step in around:
        share(step, in_group(step)).wait_recv()
        hand(in_group(step), in_group(step)).start()
    for step in range(row_groups // 2):
        theirs = lax.rem(partner + 2 * step, row_groups)
        mine = in_group(step)
        hand(mine, theirs).wait_recv()
    for step in range(row_groups // 2):
        hand(in_group(step), in_group(step)).wait_send()
    for step in around:
        share(step, place).wait_send()
    for step in across:
        left_copy(step, other(step, col)).wait_recv()
        left_copy(step, col).wait_send()
        swap(step, col).wait_send()
        cross(step).wait_send()


def exchange_kernel(
    row_groups,
    col_count,
    rows_tile,
    turned_bins,
    own_bins,
    bias,
    logits,
    landed,
    group_relay,
    col_relay,
    send_sem,
    recv_sem,
    group_recv,
    col_recv,
    group_send,
    col_send,
    own_sem,
):
    row_at = lax.axis_index("row")
    col = lax.axis_index("col")
    group = row_at // row_groups
    place = lax.rem(row_at, row_groups)
    inside = group == col
    half = row_groups // 2
    lower = place < half

    def device(to_group, to_place, to_col):
        return (to_group * row_groups + to_place, to_col)

    def remote(src, dst, send, recv, target):
        return pltpu.make_async_remote_copy(
            src_ref=src,
            dst_ref=dst,
            send_sem=send,
            recv_sem=recv,
            device_id=target,
            device_id_type=MESH,
        )

    def block(slot):
        return turned_bins.at[:, pl.ds(pl.multiple_of(slot * rows_tile, rows_tile), rows_tile), :]

    barrier = pltpu.get_barrier_semaphore()

    def greet(target):
        pl.semaphore_signal(barrier, inc=1, device_id=target, device_id_type=MESH)

    def others():
        return [lax.rem(col + step, col_count) for step in range(1, col_count)]

    def near_slot(step):
        return lax.rem(place + step, row_groups)

    @pl.when(inside)
    def _():
        for step in range(1, row_groups):
            greet(device(group, near_slot(step), col))
        for other in others():
            for index in range(half):
                greet(device(group, index, other))
                greet(device(other, half + index, col))

            @pl.when(lower)
            def _():
                greet(device(other, place, col))

            @pl.when(jnp.logical_not(lower))
            def _():
                greet(device(group, place, other))

    @pl.when(jnp.logical_not(inside))
    def _():
        @pl.when(lower)
        def _():
            for slot in range(row_groups):
                greet(device(group, slot, group))
            greet(device(col, place, col))

        @pl.when(jnp.logical_not(lower))
        def _():
            for slot in range(row_groups):
                greet(device(col, slot, col))
            greet(device(group, place, group))

    pl.semaphore_wait(
        barrier,
        jnp.where(inside, row_groups - 1 + (col_count - 1) * (row_groups + 1), row_groups + 1),
    )

    def near(slot, at):
        return remote(
            block(slot), landed.at[at], send_sem.at[slot], recv_sem.at[at], device(group, slot, col)
        )

    def by_group(index, at):
        return remote(
            block(index),
            group_relay.at[at, index],
            send_sem.at[index],
            group_recv.at[at, index],
            device(col, place, col),
        )

    def by_col(index, at):
        return remote(
            block(half + index),
            col_relay.at[at, index],
            send_sem.at[half + index],
            col_recv.at[at, index],
            device(group, place, group),
        )

    def pass_group(index, other):
        return remote(
            group_relay.at[other, index],
            landed.at[place],
            group_send.at[other, index],
            recv_sem.at[place],
            device(group, index, other),
        )

    def pass_col(index, other):
        return remote(
            col_relay.at[other, index],
            landed.at[place],
            col_send.at[other, index],
            recv_sem.at[place],
            device(other, half + index, col),
        )

    @pl.when(jnp.logical_not(inside))
    def _():
        for index in range(half):
            by_group(index, group).start()
            by_col(index, col).start()
        for slot in range(row_groups):
            remote(
                block(slot),
                landed.at[slot],
                send_sem.at[slot],
                recv_sem.at[slot],
                device(col, place, col),
            ).wait_recv()
        for index in range(half):
            by_group(index, group).wait_send()
            by_col(index, col).wait_send()

    @pl.when(inside)
    def _():
        for step in range(1, row_groups):
            near(near_slot(step), place).start()
        local = pltpu.make_async_copy(block(place), landed.at[place], own_sem)
        local.start()
        for index in range(half):
            for other in others():
                remote(
                    block(index),
                    group_relay.at[other, index],
                    send_sem.at[index],
                    group_recv.at[other, index],
                    device(other, place, col),
                ).wait_recv()
                pass_group(index, other).start()
                remote(
                    block(index),
                    col_relay.at[other, index],
                    send_sem.at[index],
                    col_recv.at[other, index],
                    device(group, place, other),
                ).wait_recv()
                pass_col(index, other).start()
        local.wait()
        for step in range(1, row_groups):
            near(near_slot(step), near_slot(step)).wait_recv()
            near(near_slot(step), place).wait_send()
        for index in range(half):
            for other in others():
                pass_group(index, other).wait_send()
                pass_col(index, other).wait_send()

    parts, lanes = landed.shape[1], landed.shape[3]
    each = lanes // rows_tile

    @pl.loop(0, parts)
    def _(part):
        got = [landed[slot, part].astype(jnp.float32) for slot in range(row_groups)]
        for inner in range(each):
            mirrored = jnp.concatenate(
                [one[:, inner * rows_tile : (inner + 1) * rows_tile] for one in got], axis=1
            )
            at = part * each + inner
            logits[at] = own_bins[at].astype(jnp.float32) + mirrored + bias[at]


def per_device(
    first_homolog_embedding,
    second_homolog_embedding,
    token_chain_index,
    incoming_pair_state,
    tensor_mixing_matrix,
    outer_product_bias,
    transition_norm_gain,
    transition_gate_weight,
    transition_up_weight,
    transition_down_weight,
    distogram_weight,
    distogram_bias,
):
    row_count = lax.axis_size("row")
    col_count = lax.axis_size("col")
    row_at = lax.axis_index("row")
    col_at = lax.axis_index("col")
    rows_tile, cols_tile, channels = incoming_pair_state.shape
    sequences, tokens_local, width = first_homolog_embedding.shape
    hid = transition_gate_weight.shape[1]
    bins_count = distogram_weight.shape[1]
    row_groups = row_count // col_count
    slab = sequences // 2
    f32, bf16 = jnp.float32, jnp.bfloat16

    vmem = pl.BlockSpec(memory_space=pltpu.VMEM)
    blocks = row_groups * col_count
    dma = pltpu.SemaphoreType.DMA
    left, right = pl.pallas_call(
        functools.partial(gather_kernel, row_groups, col_count),
        in_specs=[vmem, vmem],
        out_specs=[vmem, vmem],
        out_shape=[
            jax.ShapeDtypeStruct((col_count, tokens_local * width, sequences), bf16),
            jax.ShapeDtypeStruct((blocks, width * tokens_local, sequences), bf16),
        ],
        scratch_shapes=[
            pltpu.VMEM((col_count, width * tokens_local, sequences), bf16),
            dma((col_count,)),
            dma((col_count,)),
            dma((col_count,)),
            dma((col_count,)),
            dma((col_count,)),
            dma((col_count,)),
            dma((row_groups,)),
            dma((row_groups,)),
            dma((row_groups,)),
            dma((row_groups,)),
            dma((3,)),
        ],
        compiler_params=pltpu.CompilerParams(
            collective_id=1, has_side_effects=True, vmem_limit_bytes=VMEM_BYTES
        ),
        name="gather_tokens",
    )(
        jnp.transpose(first_homolog_embedding, (1, 2, 0)).reshape(tokens_local * width, sequences),
        jnp.transpose(second_homolog_embedding, (2, 1, 0)).reshape(width * tokens_local, sequences),
    )
    left = left.reshape(rows_tile * width, sequences)
    if tokens_local % 16:
        right = jnp.transpose(
            right.reshape(blocks, width, tokens_local, sequences), (1, 0, 2, 3)
        ).reshape(1, width * cols_tile, sequences)

    chain_rows = lax.dynamic_slice_in_dim(token_chain_index, row_at * rows_tile, rows_tile, 0)
    chain_cols = lax.dynamic_slice_in_dim(token_chain_index, col_at * cols_tile, cols_tile, 0)
    chain_cols = jnp.broadcast_to(chain_cols[:, None], (cols_tile, sequences))
    mixing = jnp.transpose(
        tensor_mixing_matrix.reshape(width, width, channels), (2, 1, 0)
    ).reshape(channels, width * width)
    bias = jnp.broadcast_to(outer_product_bias[:, None], (channels, cols_tile))
    gain = jnp.broadcast_to(transition_norm_gain[:, None], (channels, cols_tile))
    gate_up = jnp.concatenate([transition_gate_weight.T, transition_up_weight.T], axis=0)

    group = min(16, rows_tile)
    lanes = 128
    parts = bins_count * rows_tile // lanes

    def whole(*shape):
        return pl.BlockSpec(shape, lambda step: (0,) * len(shape))

    pair_out, own_bins, turned_bins = pl.pallas_call(
        functools.partial(pair_kernel, slab, width, group, rows_tile),
        grid=(rows_tile // group,),
        in_specs=[
            pl.BlockSpec(memory_space=pltpu.SMEM),
            whole(cols_tile, sequences),
            pl.BlockSpec((group * width, sequences), lambda step: (step, 0)),
            whole(*right.shape),
            pl.BlockSpec((group, cols_tile, channels), lambda step: (step, 0, 0)),
            whole(channels, width * width),
            whole(channels, cols_tile),
            whole(channels, cols_tile),
            whole(2 * hid, channels),
            whole(channels, hid),
            whole(bins_count, channels),
        ],
        out_specs=[
            pl.BlockSpec((group, cols_tile, channels), lambda step: (step, 0, 0)),
            whole(bins_count, rows_tile, cols_tile),
            whole(parts, cols_tile, lanes),
        ],
        out_shape=[
            jax.ShapeDtypeStruct((rows_tile, cols_tile, channels), bf16),
            jax.ShapeDtypeStruct((bins_count, rows_tile, cols_tile), bf16),
            jax.ShapeDtypeStruct((parts, cols_tile, lanes), bf16),
        ],
        scratch_shapes=[
            pltpu.VMEM((group * width, 2 * sequences), bf16),
            pltpu.VMEM((cols_tile, 2 * sequences), bf16),
            pltpu.VMEM((group, width * width, cols_tile), bf16),
            pltpu.VMEM((cols_tile // lanes, bins_count * rows_tile, lanes), f32),
        ],
        compiler_params=pltpu.CompilerParams(vmem_limit_bytes=VMEM_BYTES),
        name="pair_tile",
    )(
        chain_rows,
        chain_cols,
        left,
        right,
        incoming_pair_state,
        mixing,
        bias,
        gain,
        gate_up,
        transition_down_weight.T,
        distogram_weight.T,
    )

    half = row_groups // 2
    logits = pl.pallas_call(
        functools.partial(exchange_kernel, row_groups, col_count, rows_tile),
        in_specs=[vmem, vmem, pl.BlockSpec(memory_space=pltpu.SMEM)],
        out_specs=vmem,
        out_shape=jax.ShapeDtypeStruct((bins_count, rows_tile, cols_tile), f32),
        scratch_shapes=[
            pltpu.VMEM((row_groups, parts, rows_tile, lanes), bf16),
            pltpu.VMEM((col_count, half, parts, rows_tile, lanes), bf16),
            pltpu.VMEM((col_count, half, parts, rows_tile, lanes), bf16),
            dma((row_groups,)),
            dma((row_groups,)),
            dma((col_count, half)),
            dma((col_count, half)),
            dma((col_count, half)),
            dma((col_count, half)),
            dma,
        ],
        compiler_params=pltpu.CompilerParams(
            collective_id=0, has_side_effects=True, vmem_limit_bytes=VMEM_BYTES
        ),
        name="mirror_bins",
    )(turned_bins, own_bins, distogram_bias)
    return (pair_out, logits)


def solution(mesh):
    placed = (
        P(None, ("row", "col"), None),
        P(None, ("row", "col"), None),
        P(),
        P("row", "col", None),
        P(),
        P(),
        P(),
        P(),
        P(),
        P(),
        P(),
        P(),
    )
    return jax.shard_map(
        per_device,
        mesh=mesh,
        in_specs=placed,
        out_specs=(P("row", "col", None), P(None, "row", "col")),
        check_vma=False,
    )
```

```python
import functools

import jax
import jax.numpy as jnp
from jax import lax
from jax.experimental import pallas as pl
from jax.experimental.pallas import tpu as pltpu
from jax.sharding import PartitionSpec as P

MESH = pl.DeviceIdType.MESH
VMEM_BYTES = 56 * 1024 * 1024


def pair_kernel(
    slab,
    width,
    group,
    rows_tile,
    chain_all,
    chain_line,
    left,
    right,
    incoming,
    mixing,
    bias_line,
    gain_line,
    gate_weight,
    up_weight,
    down_weight,
    bins_weight_in,
    pair_out,
    own_bins,
    turned_bins,
    lhs,
    weights,
    outer,
    bins,
    chain_cols,
    bias,
    gain,
    gate_up,
    down,
    bins_weight,
):
    step = pl.program_id(0)
    cols_tile = chain_cols.shape[0]
    sequences = 2 * slab
    channels = mixing.shape[0]
    hid = down.shape[1]
    bins_count = bins_weight.shape[0]
    sides, _, lanes = bins.shape
    first_row = step * group
    row_base = lax.axis_index("row") * rows_tile + first_row
    first_chain = chain_all[row_base]
    last_chain = chain_all[row_base + group - 1]

    def turned(value):
        return value.astype(jnp.float32).T

    @pl.when(step == 0)
    def _():
        start = pl.multiple_of(lax.axis_index("col") * cols_tile, cols_tile)
        line = chain_line[:, pl.ds(start, cols_tile)].astype(jnp.float32)
        chain_cols[...] = jnp.broadcast_to(line, (sequences, cols_tile)).T
        bias[...] = jnp.broadcast_to(bias_line[...], (cols_tile, channels)).T
        gain[...] = jnp.broadcast_to(gain_line[...], (cols_tile, channels)).T
        gate_up[:hid] = turned(gate_weight[...]).astype(jnp.bfloat16)
        gate_up[hid:] = turned(up_weight[...]).astype(jnp.bfloat16)
        down[...] = turned(down_weight[...]).astype(jnp.bfloat16)
        bins_weight[...] = turned(bins_weight_in[...]).astype(jnp.bfloat16)

    def load_chains(low):
        lane = lax.broadcasted_iota(jnp.int32, (cols_tile, sequences), 1)
        apart = jnp.where(lane < slab, 1.0 / slab, 0.0).astype(jnp.float32)
        for half in range(2):
            chain = low + half
            same = chain_cols[...] == chain.astype(jnp.float32)
            weights[:, half * sequences : (half + 1) * sequences] = jnp.where(
                same, 0.5 / slab, apart
            ).astype(jnp.bfloat16)
            for row in range(group):
                keep = jnp.where(chain_all[row_base + row] == chain, 1.0, 0.0)
                lhs[row * width : (row + 1) * width, half * sequences : (half + 1) * sequences] = (
                    left[row * width : (row + 1) * width, :].astype(jnp.float32) * keep
                ).astype(jnp.bfloat16)

    def outer_part(depth):
        tokens = right.shape[1] // width
        block = right[:, pl.ds(pl.multiple_of(depth * tokens, tokens), tokens), :]
        block = block.reshape(cols_tile, sequences)
        spread = jnp.concatenate([block, block], axis=1) * weights[...]
        part = lax.dot_general(
            lhs[...], spread, (((1,), (1,)), ((), ())), preferred_element_type=jnp.float32
        )
        return part.astype(jnp.bfloat16).reshape(group, width, cols_tile)

    def place(depth):
        return pl.ds(pl.multiple_of(depth * width, width), width)

    load_chains(first_chain)

    @pl.loop(0, width, unroll=8)
    def _(depth):
        outer[:, place(depth), :] = outer_part(depth)

    @pl.loop(1, (last_chain - first_chain) // 2 + 1)
    def _(turn):
        load_chains(first_chain + 2 * turn)

        @pl.loop(0, width)
        def _(depth):
            outer[:, place(depth), :] = outer[:, place(depth), :] + outer_part(depth)

    def one_row(row):
        mid = jnp.dot(mixing[...], outer[row], preferred_element_type=jnp.float32)
        mid = mid + bias[...] + incoming[row].astype(jnp.float32).T
        mid = mid.astype(jnp.bfloat16).astype(jnp.float32)
        center = jnp.mean(mid, axis=0, keepdims=True)
        shifted = mid - center
        spread = jnp.mean(shifted * shifted, axis=0, keepdims=True)
        normed = (shifted * lax.rsqrt(spread + 1e-05) * gain[...]).astype(jnp.bfloat16)
        both = jnp.dot(gate_up[...], normed, preferred_element_type=jnp.float32)
        half_gate = 0.5 * both[:hid]
        hidden = ((half_gate + half_gate * jnp.tanh(half_gate)) * both[hid:]).astype(jnp.bfloat16)
        result = mid + jnp.dot(down[...], hidden, preferred_element_type=jnp.float32)
        rounded = result.astype(jnp.bfloat16)
        pair_out[row] = result.T.astype(jnp.bfloat16)
        projected = jnp.dot(bins_weight[...], rounded, preferred_element_type=jnp.float32)
        for side in range(sides):
            bins[side, pl.ds(first_row + row, bins_count, stride=rows_tile), :] = projected[
                :, side * lanes : (side + 1) * lanes
            ]

    @pl.loop(0, group // 4)
    def _(quad):
        for part in range(4):
            one_row(4 * quad + part)

    @pl.when(step == pl.num_programs(0) - 1)
    def _():
        for side in range(sides):
            columns = slice(side * lanes, (side + 1) * lanes)
            own_bins[:, :, columns] = (
                bins[side].astype(jnp.bfloat16).reshape(bins_count, rows_tile, lanes)
            )
            for part in range(turned_bins.shape[0]):
                turned_bins[part, columns, :] = bins[
                    side, part * lanes : (part + 1) * lanes, :
                ].T.astype(jnp.bfloat16)


def gather_kernel(
    row_groups,
    col_count,
    first,
    second,
    left,
    right,
    crossed,
    left_send,
    left_recv,
    cross_send,
    cross_recv,
    swap_send,
    swap_recv,
    group_send,
    group_recv,
    core_send,
    core_recv,
    own_sem,
):
    row_at = lax.axis_index("row")
    col = lax.axis_index("col")
    group = row_at // row_groups
    place = lax.rem(row_at, row_groups)
    partner = place + 1 - 2 * lax.rem(place, 2)

    def device(to_group, to_place, to_col):
        return (to_group * row_groups + to_place, to_col)

    def other(step, at):
        return lax.rem(at + step, col_count)

    def in_group(step):
        return lax.rem(place + 2 * step, row_groups)

    def remote(src, dst, send, recv, target):
        return pltpu.make_async_remote_copy(
            src_ref=src,
            dst_ref=dst,
            send_sem=send,
            recv_sem=recv,
            device_id=target,
            device_id_type=MESH,
        )

    def run(at):
        return right.at[pl.ds(at * col_count, col_count)]

    across = range(1, col_count)
    around = range(1, row_groups // 2)
    barrier = pltpu.get_barrier_semaphore()
    for step in across:
        for target in (device(other(step, group), place, col), device(group, place, other(step, col))):
            pl.semaphore_signal(barrier, inc=1, device_id=target, device_id_type=MESH)
    for step in around:
        pl.semaphore_signal(
            barrier, inc=1, device_id=device(group, in_group(step), col), device_id_type=MESH
        )
    pl.semaphore_signal(
        barrier, inc=1, device_id=device(group, partner, col), device_id_type=MESH
    )
    pl.semaphore_wait(barrier, 2 * (col_count - 1) + row_groups // 2)

    def cross(step):
        to = other(step, group)
        return remote(
            second, crossed.at[group], cross_send.at[to], cross_recv.at[group], device(to, place, col)
        )

    def crossing(source):
        return remote(
            second,
            crossed.at[source],
            cross_send.at[source],
            cross_recv.at[source],
            device(source, place, col),
        )

    def left_copy(step, at):
        to = other(step, col)
        return remote(
            first, left.at[at], left_send.at[to], left_recv.at[at], device(group, place, to)
        )

    def swap(step, at):
        to = other(step, col)
        return remote(
            crossed.at[to],
            right.at[place * col_count + at],
            swap_send.at[to],
            swap_recv.at[at],
            device(group, place, to),
        )

    def share(step, at):
        to = in_group(step)
        return remote(
            run(at), run(at), group_send.at[to], group_recv.at[at], device(group, to, col)
        )

    def hand(mine, theirs):
        return remote(
            run(mine),
            run(theirs),
            core_send.at[mine],
            core_recv.at[theirs],
            device(group, partner, col),
        )

    for step in across:
        cross(step).start()
    own = pltpu.make_async_copy(second, crossed.at[group], own_sem.at[0])
    own.start()
    own_left = pltpu.make_async_copy(first, left.at[col], own_sem.at[1])
    own_left.start()
    own.wait()
    own_left.wait()
    for step in across:
        left_copy(step, col).start()

    for step in range(col_count):
        wanted = other(step, group)
        if step:
            crossing(wanted).wait_recv()

        @pl.when(wanted != col)
        def _():
            remote(
                crossed.at[wanted],
                right.at[place * col_count + col],
                swap_send.at[wanted],
                swap_recv.at[col],
                device(group, place, wanted),
            ).start()

        @pl.when(wanted == col)
        def _():
            kept = pltpu.make_async_copy(
                crossed.at[wanted], right.at[place * col_count + col], own_sem.at[2]
            )
            kept.start()
            kept.wait()

    for step in across:
        swap(step, other(step, col)).wait_recv()
    for step in around:
        share(step, place).start()
    hand(place, place).start()
    for step in around:
        share(step, in_group(step)).wait_recv()
        hand(in_group(step), in_group(step)).start()
    for step in range(row_groups // 2):
        theirs = lax.rem(partner + 2 * step, row_groups)
        mine = in_group(step)
        hand(mine, theirs).wait_recv()
    for step in range(row_groups // 2):
        hand(in_group(step), in_group(step)).wait_send()
    for step in around:
        share(step, place).wait_send()
    for step in across:
        left_copy(step, other(step, col)).wait_recv()
        left_copy(step, col).wait_send()
        swap(step, col).wait_send()
        cross(step).wait_send()


def exchange_kernel(
    row_groups,
    col_count,
    rows_tile,
    turned_bins,
    landed,
    group_relay,
    col_relay,
    send_sem,
    recv_sem,
    group_recv,
    col_recv,
    group_send,
    col_send,
    own_sem,
):
    row_at = lax.axis_index("row")
    col = lax.axis_index("col")
    group = row_at // row_groups
    place = lax.rem(row_at, row_groups)
    inside = group == col
    half = row_groups // 2
    lower = place < half

    def device(to_group, to_place, to_col):
        return (to_group * row_groups + to_place, to_col)

    def remote(src, dst, send, recv, target):
        return pltpu.make_async_remote_copy(
            src_ref=src,
            dst_ref=dst,
            send_sem=send,
            recv_sem=recv,
            device_id=target,
            device_id_type=MESH,
        )

    def block(slot):
        return turned_bins.at[:, pl.ds(pl.multiple_of(slot * rows_tile, rows_tile), rows_tile), :]

    barrier = pltpu.get_barrier_semaphore()

    def greet(target):
        pl.semaphore_signal(barrier, inc=1, device_id=target, device_id_type=MESH)

    def others():
        return [lax.rem(col + step, col_count) for step in range(1, col_count)]

    def near_slot(step):
        return lax.rem(place + step, row_groups)

    @pl.when(inside)
    def _():
        for step in range(1, row_groups):
            greet(device(group, near_slot(step), col))
        for other in others():
            for index in range(half):
                greet(device(group, index, other))
                greet(device(other, half + index, col))

            @pl.when(lower)
            def _():
                greet(device(other, place, col))

            @pl.when(jnp.logical_not(lower))
            def _():
                greet(device(group, place, other))

    @pl.when(jnp.logical_not(inside))
    def _():
        @pl.when(lower)
        def _():
            for slot in range(row_groups):
                greet(device(group, slot, group))
            greet(device(col, place, col))

        @pl.when(jnp.logical_not(lower))
        def _():
            for slot in range(row_groups):
                greet(device(col, slot, col))
            greet(device(group, place, group))

    pl.semaphore_wait(
        barrier,
        jnp.where(inside, row_groups - 1 + (col_count - 1) * (row_groups + 1), row_groups + 1),
    )

    def near(slot, at):
        return remote(
            block(slot), landed.at[at], send_sem.at[slot], recv_sem.at[at], device(group, slot, col)
        )

    def by_group(index, at):
        return remote(
            block(index),
            group_relay.at[at, index],
            send_sem.at[index],
            group_recv.at[at, index],
            device(col, place, col),
        )

    def by_col(index, at):
        return remote(
            block(half + index),
            col_relay.at[at, index],
            send_sem.at[half + index],
            col_recv.at[at, index],
            device(group, place, group),
        )

    def pass_group(index, other):
        return remote(
            group_relay.at[other, index],
            landed.at[place],
            group_send.at[other, index],
            recv_sem.at[place],
            device(group, index, other),
        )

    def pass_col(index, other):
        return remote(
            col_relay.at[other, index],
            landed.at[place],
            col_send.at[other, index],
            recv_sem.at[place],
            device(other, half + index, col),
        )

    @pl.when(jnp.logical_not(inside))
    def _():
        for index in range(half):
            by_group(index, group).start()
            by_col(index, col).start()
        for slot in range(row_groups):
            remote(
                block(slot),
                landed.at[slot],
                send_sem.at[slot],
                recv_sem.at[slot],
                device(col, place, col),
            ).wait_recv()
        for index in range(half):
            by_group(index, group).wait_send()
            by_col(index, col).wait_send()

    @pl.when(inside)
    def _():
        local = pltpu.make_async_copy(block(place), landed.at[place], own_sem)
        local.start()
        for step in range(1, row_groups):
            near(near_slot(step), place).start()
        for index in range(half):
            for other in others():
                remote(
                    block(index),
                    group_relay.at[other, index],
                    send_sem.at[index],
                    group_recv.at[other, index],
                    device(other, place, col),
                ).wait_recv()
                pass_group(index, other).start()
                remote(
                    block(index),
                    col_relay.at[other, index],
                    send_sem.at[index],
                    col_recv.at[other, index],
                    device(group, place, other),
                ).wait_recv()
                pass_col(index, other).start()
        local.wait()
        for step in range(1, row_groups):
            near(near_slot(step), near_slot(step)).wait_recv()
            near(near_slot(step), place).wait_send()
        for index in range(half):
            for other in others():
                pass_group(index, other).wait_send()
                pass_col(index, other).wait_send()

def add_kernel(own_bins, landed, bias, logits):
    row_groups, parts, rows_tile, lanes = landed.shape
    each = lanes // rows_tile
    first = pl.program_id(0) * parts * each

    @pl.loop(0, parts)
    def _(part):
        got = [landed[slot, part].astype(jnp.float32) for slot in range(row_groups)]
        for inner in range(each):
            mirrored = jnp.concatenate(
                [one[:, inner * rows_tile : (inner + 1) * rows_tile] for one in got], axis=1
            )
            at = part * each + inner
            logits[at] = own_bins[at].astype(jnp.float32) + mirrored + bias[first + at]


def per_device(
    first_homolog_embedding,
    second_homolog_embedding,
    token_chain_index,
    incoming_pair_state,
    tensor_mixing_matrix,
    outer_product_bias,
    transition_norm_gain,
    transition_gate_weight,
    transition_up_weight,
    transition_down_weight,
    distogram_weight,
    distogram_bias,
):
    row_count = lax.axis_size("row")
    col_count = lax.axis_size("col")
    rows_tile, cols_tile, channels = incoming_pair_state.shape
    sequences, tokens_local, width = first_homolog_embedding.shape
    hid = transition_gate_weight.shape[1]
    bins_count = distogram_weight.shape[1]
    row_groups = row_count // col_count
    slab = sequences // 2
    f32, bf16 = jnp.float32, jnp.bfloat16

    vmem = pl.BlockSpec(memory_space=pltpu.VMEM)
    blocks = row_groups * col_count
    dma = pltpu.SemaphoreType.DMA
    left, right = pl.pallas_call(
        functools.partial(gather_kernel, row_groups, col_count),
        in_specs=[vmem, vmem],
        out_specs=[vmem, vmem],
        out_shape=[
            jax.ShapeDtypeStruct((col_count, tokens_local * width, sequences), bf16),
            jax.ShapeDtypeStruct((blocks, width * tokens_local, sequences), bf16),
        ],
        scratch_shapes=[
            pltpu.VMEM((col_count, width * tokens_local, sequences), bf16),
            dma((col_count,)),
            dma((col_count,)),
            dma((col_count,)),
            dma((col_count,)),
            dma((col_count,)),
            dma((col_count,)),
            dma((row_groups,)),
            dma((row_groups,)),
            dma((row_groups,)),
            dma((row_groups,)),
            dma((3,)),
        ],
        compiler_params=pltpu.CompilerParams(
            collective_id=1, has_side_effects=True, vmem_limit_bytes=VMEM_BYTES
        ),
        name="gather_tokens",
    )(
        jnp.transpose(first_homolog_embedding, (1, 2, 0)).reshape(tokens_local * width, sequences),
        jnp.transpose(second_homolog_embedding, (2, 1, 0)).reshape(width * tokens_local, sequences),
    )
    left = left.reshape(rows_tile * width, sequences)
    if tokens_local % 16:
        right = jnp.transpose(
            right.reshape(blocks, width, tokens_local, sequences), (1, 0, 2, 3)
        ).reshape(1, width * cols_tile, sequences)

    mixing = jnp.transpose(
        tensor_mixing_matrix.reshape(width, width, channels), (2, 1, 0)
    ).reshape(channels, width * width)
    group = min(16, rows_tile)
    lanes = 128
    parts = bins_count * rows_tile // lanes

    def whole(*shape):
        return pl.BlockSpec(shape, lambda step: (0,) * len(shape))

    pair_out, own_bins, turned_bins = pl.pallas_call(
        functools.partial(pair_kernel, slab, width, group, rows_tile),
        grid=(rows_tile // group,),
        in_specs=[
            pl.BlockSpec(memory_space=pltpu.SMEM),
            whole(1, token_chain_index.shape[0]),
            pl.BlockSpec((group * width, sequences), lambda step: (step, 0)),
            whole(*right.shape),
            pl.BlockSpec((group, cols_tile, channels), lambda step: (step, 0, 0)),
            whole(channels, width * width),
            whole(1, channels),
            whole(1, channels),
            whole(channels, hid),
            whole(channels, hid),
            whole(hid, channels),
            whole(channels, bins_count),
        ],
        out_specs=[
            pl.BlockSpec((group, cols_tile, channels), lambda step: (step, 0, 0)),
            whole(bins_count, rows_tile, cols_tile),
            whole(parts, cols_tile, lanes),
        ],
        out_shape=[
            jax.ShapeDtypeStruct((rows_tile, cols_tile, channels), bf16),
            jax.ShapeDtypeStruct((bins_count, rows_tile, cols_tile), bf16),
            jax.ShapeDtypeStruct((parts, cols_tile, lanes), bf16),
        ],
        scratch_shapes=[
            pltpu.VMEM((group * width, 2 * sequences), bf16),
            pltpu.VMEM((cols_tile, 2 * sequences), bf16),
            pltpu.VMEM((group, width * width, cols_tile), bf16),
            pltpu.VMEM((cols_tile // lanes, bins_count * rows_tile, lanes), f32),
            pltpu.VMEM((cols_tile, sequences), f32),
            pltpu.VMEM((channels, cols_tile), f32),
            pltpu.VMEM((channels, cols_tile), f32),
            pltpu.VMEM((2 * hid, channels), bf16),
            pltpu.VMEM((channels, hid), bf16),
            pltpu.VMEM((bins_count, channels), bf16),
        ],
        compiler_params=pltpu.CompilerParams(vmem_limit_bytes=VMEM_BYTES),
        name="pair_tile",
    )(
        token_chain_index,
        token_chain_index[None, :],
        left,
        right,
        incoming_pair_state,
        mixing,
        outer_product_bias[None, :],
        transition_norm_gain[None, :],
        transition_gate_weight,
        transition_up_weight,
        transition_down_weight,
        distogram_weight,
    )

    half = row_groups // 2
    landed = pl.pallas_call(
        functools.partial(exchange_kernel, row_groups, col_count, rows_tile),
        in_specs=[vmem],
        out_specs=vmem,
        out_shape=jax.ShapeDtypeStruct((row_groups, parts, rows_tile, lanes), bf16),
        scratch_shapes=[
            pltpu.VMEM((col_count, half, parts, rows_tile, lanes), bf16),
            pltpu.VMEM((col_count, half, parts, rows_tile, lanes), bf16),
            dma((row_groups,)),
            dma((row_groups,)),
            dma((col_count, half)),
            dma((col_count, half)),
            dma((col_count, half)),
            dma((col_count, half)),
            dma,
        ],
        compiler_params=pltpu.CompilerParams(
            collective_id=0, has_side_effects=True, vmem_limit_bytes=VMEM_BYTES
        ),
        name="mirror_bins",
    )(turned_bins)
    steps = 4
    logits = pl.pallas_call(
        add_kernel,
        grid=(steps,),
        in_specs=[
            pl.BlockSpec((bins_count // steps, rows_tile, cols_tile), lambda step: (step, 0, 0)),
            pl.BlockSpec(
                (row_groups, parts // steps, rows_tile, lanes), lambda step: (0, step, 0, 0)
            ),
            pl.BlockSpec(memory_space=pltpu.SMEM),
        ],
        out_specs=pl.BlockSpec(
            (bins_count // steps, rows_tile, cols_tile), lambda step: (step, 0, 0)
        ),
        out_shape=jax.ShapeDtypeStruct((bins_count, rows_tile, cols_tile), f32),
        compiler_params=pltpu.CompilerParams(vmem_limit_bytes=VMEM_BYTES),
        name="add_bins",
    )(own_bins, landed, distogram_bias)
    return (pair_out, logits)


def solution(mesh):
    placed = (
        P(None, ("row", "col"), None),
        P(None, ("row", "col"), None),
        P(),
        P("row", "col", None),
        P(),
        P(),
        P(),
        P(),
        P(),
        P(),
        P(),
        P(),
    )
    return jax.shard_map(
        per_device,
        mesh=mesh,
        in_specs=placed,
        out_specs=(P("row", "col", None), P(None, "row", "col")),
        check_vma=False,
    )
```
